32 devices in a mesh: group: 2 (over y), dp: 8 (over z, x), tensor: 2 (over core).
Axes of the slice: x: 2, y: 2, z: 4, core: 2. Of those that a mesh axis runs over, the one named last changes fastest.
Arguments:
- roll_inputs: bfloat16 [64, 128, 14336], P(('group', 'dp'), None, 'tensor'), parts along dimension 0, may hold values from -6 to 6
- roll_grads: bfloat16 [64, 128, 8192], P(('group', 'dp'), None, 'tensor'), parts along dimension 0, may hold values from -6 to 6
- ref_inputs: bfloat16 [16, 128, 14336], P(('group', 'dp'), None, 'tensor'), parts along dimension 0, may hold values from -6 to 6
- ref_grads: bfloat16 [16, 128, 8192], P(('group', 'dp'), None, 'tensor'), parts along dimension 0, may hold values from -6 to 6
- in_basis: bfloat16 [14336, 64], P('tensor'), may hold values from -0.046875 to 0.046875
- out_basis: bfloat16 [8192, 64], P('tensor'), may hold values from -0.0625 to 0.0625
- roll_lengths: int32 [64], P(('group', 'dp')), parts along dimension 0, may hold values from 1 to 128, 2112 in all
- ref_lengths: int32 [16], P(('group', 'dp')), parts along dimension 0, may hold values from 1 to 128, 576 in all
Outputs:
- scores: float32 [64, 8], P(('group', 'dp')), parts along dimension 0
The draws below stay inside these ranges and needn't reach their ends.
There are 2 independent parts, one for each index of `group`. The reference program is written for one: setup_inputs(seed, part) draws one part's arguments, and reference() takes and returns one part's arrays. A program takes and returns all parts, laid end to end along the dimension named above; an argument that names none is the same for every part. Nothing has to cross between parts.
Inputs may be any that keep to these rules, and one draw needn't show every extreme that they name: `roll_lengths`: positions at or beyond a rollout's length are padding; some rollout has exactly 128 tokens. `ref_lengths`: positions at or beyond a reference prompt's length are padding; some reference prompt has exactly 128 tokens.
All inputs are finite; a program needn't handle non-finite values. No bound on the sum of `roll_lengths` or of `ref_lengths` on one device may be relied on, other than what follows from the above.
Results may differ from the reference program's by a relative error of at most 0.0003.
Values sent between devices are 32-bit elements; how exact they have to be, the bound alone decides.
No kernel may reach another device: no remote copies, remote signals or barrier semaphores. Data moves between devices by JAX's collectives and lax.ppermute only.
A program may use at most 64 MiB of HBM per device.

```python
import math
import jax
import jax.numpy as jnp
import numpy as np
from jax import lax

D = 8192
HID = 14336
KI = 64
KO = 64
LEN = 128
ROLLOUTS = 32
REFS = 8


def level_of(own_key, dims, pieces, low, largest):
    loudness = 1.0
    for axis_at, shards_of in pieces:
        heights = jax.random.uniform(jax.random.fold_in(jax.random.fold_in(own_key, 6), axis_at), (shards_of,), jnp.float32, low / len(pieces), largest / len(pieces))
        loudness = loudness * jnp.repeat(jnp.exp(heights), dims[axis_at] // shards_of).reshape((-1,) + (1,) * (len(dims) - 1 - axis_at))
    return loudness


def length_profile(amount, total, limit, skew):
    portions = [(1 << 20) // math.isqrt(grade ** skew) + 1 for grade in range(2, amount + 1)]
    surplus, given = total - limit - (amount - 1), [1] * (amount - 1)
    while surplus > 0:
        movable = [i for i in range(amount - 1) if given[i] < limit]
        mass, left = sum([portions[i] for i in movable]), surplus
        for i in movable:
            extra = min(limit - given[i], max(1, left * portions[i] // mass), surplus)
            given[i] = given[i] + extra
            surplus = surplus - extra
    return np.array([limit] + given)


def uneven(own_key, amount, total, limit, slope):
    if amount == 2:
        one = jax.random.randint(own_key, (), max(1, total - limit), min(limit, total - 1) + 1)
        return jnp.stack([one, total - one])
    sizes = jnp.asarray(length_profile(amount, total, limit, slope), jnp.int32)
    couples = (amount - 1) // 2
    donor, taker = sizes[1:1 + 2 * couples:2], sizes[2:2 + 2 * couples:2]
    margin = jnp.minimum(donor - 1, limit - taker)
    moved = jax.random.randint(jax.random.fold_in(own_key, 1), (couples,), 0, 1 << 20) % (margin + 1)
    sizes = sizes.at[1:1 + 2 * couples:2].set(donor - moved).at[2:2 + 2 * couples:2].set(taker + moved)
    return sizes[jax.random.permutation(jax.random.fold_in(own_key, 2), amount)]


def noise(own_key, shape, deviation, bound, pieces=(), kind=jnp.bfloat16):
    entries = jax.random.normal(own_key, shape, jnp.float32) * deviation
    if len(pieces) > 0:
        entries = level_of(own_key, shape, pieces, -0.22, 0.18) * entries
    return jnp.clip(entries, min=-bound, max=bound).astype(kind)


def setup_inputs(seed: int = 0, part: int = 0) -> dict:
    arg_keys = jax.random.split(jax.random.key(seed), 9)
    part_keys = jax.random.split(jax.random.fold_in(arg_keys[8], part), 9)
    roll_inputs = noise(part_keys[0], (ROLLOUTS, LEN, HID), 1.0, 6.0, ((0, 8), (2, 2)))
    roll_grads = noise(part_keys[1], (ROLLOUTS, LEN, D), 1.0, 6.0, ((0, 8), (2, 2)))
    ref_inputs = noise(part_keys[2], (REFS, LEN, HID), 1.0, 6.0, ((0, 8), (2, 2)))
    ref_grads = noise(part_keys[3], (REFS, LEN, D), 1.0, 6.0, ((0, 8), (2, 2)))
    in_basis = noise(arg_keys[4], (HID, KI), HID ** -0.5, 0.046875, ((0, 2),))
    out_basis = noise(arg_keys[5], (D, KO), D ** -0.5, 0.0625, ((0, 2),))
    roll_lengths = uneven(part_keys[6], ROLLOUTS, ROLLOUTS * LEN // 2 + LEN // 2, LEN, 1).astype(jnp.int32)
    ref_lengths = uneven(part_keys[7], REFS, REFS * LEN // 2 + LEN // 2, LEN, 1).astype(jnp.int32)
    return {"roll_inputs": roll_inputs, "roll_grads": roll_grads, "ref_inputs": ref_inputs, "ref_grads": ref_grads, "in_basis": in_basis, "out_basis": out_basis, "roll_lengths": roll_lengths, "ref_lengths": ref_lengths}


def make_units(inputs, grads, lengths, in_basis, out_basis):
    rows = inputs.shape[0]
    span = inputs.shape[1]
    xp = jnp.dot(inputs.reshape(rows * span, inputs.shape[2]), in_basis, preferred_element_type=jnp.float32).reshape(rows, span, in_basis.shape[1])
    gp = jnp.dot(grads.reshape(rows * span, grads.shape[2]), out_basis, preferred_element_type=jnp.float32).reshape(rows, span, out_basis.shape[1])
    positions = jnp.arange(span, dtype=jnp.int32)
    keep = (positions[None, :] < lengths[:, None]).astype(jnp.float32)
    gp = gp * keep[:, :, None]
    sketch = jnp.einsum('rto,rti->roi', gp, xp, precision=lax.Precision.HIGHEST).reshape(rows, -1)
    spread = jnp.sqrt(lax.optimization_barrier(jnp.mean(sketch * sketch, axis=1, keepdims=True)) + 1e-06)
    return sketch / spread

def reference(roll_inputs, roll_grads, ref_inputs, ref_grads, in_basis, out_basis, roll_lengths, ref_lengths):
    roll_units = make_units(roll_inputs, roll_grads, roll_lengths, in_basis, out_basis)
    ref_units = make_units(ref_inputs, ref_grads, ref_lengths, in_basis, out_basis)
    raw = jnp.dot(roll_units, ref_units.T, preferred_element_type=jnp.float32, precision=lax.Precision.HIGHEST)
    return raw / jnp.sqrt(jnp.float32(KO * KI))
```

```python
import functools
import math

import jax
import jax.numpy as jnp
from jax import lax
from jax.experimental import pallas as pl
from jax.experimental.pallas import tpu as pltpu
from jax.sharding import PartitionSpec as P

BLOCK = 16
TILE = 128
ROOM = 63 << 20
EXACT = lax.Precision.HIGHEST


def columns(width):
    step = 1024 if width % 1024 == 0 else width
    return [(at, step) for at in range(0, width, step)]


def times_basis(rows, basis):
    return lax.dot_general(
        rows, basis, (((1,), (1,)), ((), ())), preferred_element_type=jnp.float32
    )


def ref_kernel(x_hbm, g_hbm, bx_hbm, bg_hbm, len_hbm, z_ref, x, g, bx, bg, lens, sems, len_sem):
    len_copy = pltpu.make_async_copy(len_hbm, lens, len_sem)
    len_copy.start()
    work = []
    for part, (src, basis_src, dst, basis_dst) in enumerate(
        ((x_hbm, bx_hbm, x, bx), (g_hbm, bg_hbm, g, bg))
    ):
        for at, step in columns(src.shape[2]):
            cut = pl.ds(at, step)
            k = len(work)
            copies = (
                pltpu.make_async_copy(basis_src.at[:, cut], basis_dst.at[:, cut], sems.at[0, k]),
                pltpu.make_async_copy(src.at[0, :, cut], dst.at[:, cut], sems.at[1, k]),
            )
            for copy in copies:
                copy.start()
            work.append((part, dst, basis_dst, cut, copies))
    sums = [None, None]
    for part, rows, basis, cut, copies in work:
        for copy in copies:
            copy.wait()
        term = times_basis(rows[:, cut], basis[:, cut])
        sums[part] = term if sums[part] is None else sums[part] + term
    len_copy.wait()
    keep = lax.broadcasted_iota(jnp.int32, sums[1].shape, 0) < lens[0]
    z_ref[...] = jnp.concatenate([jnp.where(keep, sums[1], 0.0), sums[0]], axis=1)


def project_ref(x, g, bx, bg, lengths):
    span, wide_x, wide_g = x.shape[1], x.shape[2], g.shape[2]
    parts = len(columns(wide_x)) + len(columns(wide_g))
    return pl.pallas_call(
        ref_kernel,
        out_shape=jax.ShapeDtypeStruct((span, bx.shape[0] + bg.shape[0]), jnp.float32),
        in_specs=[pl.BlockSpec(memory_space=pltpu.HBM)] * 5,
        out_specs=pl.BlockSpec(memory_space=pltpu.VMEM),
        scratch_shapes=[
            pltpu.VMEM((span, wide_x), x.dtype),
            pltpu.VMEM((span, wide_g), g.dtype),
            pltpu.VMEM(bx.shape, bx.dtype),
            pltpu.VMEM(bg.shape, bg.dtype),
            pltpu.SMEM(lengths.shape, jnp.int32),
            pltpu.SemaphoreType.DMA((2, parts)),
            pltpu.SemaphoreType.DMA,
        ],
        compiler_params=pltpu.CompilerParams(vmem_limit_bytes=ROOM),
        cost_estimate=pl.CostEstimate(
            flops=2 * span * (wide_x + wide_g) * 64, bytes_accessed=5 << 20, transcendentals=0
        ),
    )(x, g, bx, bg, lengths)


def sketch_of(z):
    half = z.shape[1] // 2
    full = lax.dot_general(
        z[:, :half], z[:, half:], (((0,), (0,)), ((), ())),
        preferred_element_type=jnp.float32, precision=EXACT,
    )
    rows = half // 2
    return jnp.concatenate([full[:rows], full[rows:]], axis=1)


def sketch_kernel(own_ref, other_ref, sketch_ref):
    sketch_ref[...] = sketch_of(own_ref[...] + other_ref[...])


def ref_sketch(own, other):
    half = own.shape[1] // 2
    return pl.pallas_call(
        sketch_kernel,
        out_shape=jax.ShapeDtypeStruct((half // 2, half * 2), jnp.float32),
        in_specs=[pl.BlockSpec(memory_space=pltpu.VMEM)] * 2,
        out_specs=pl.BlockSpec(memory_space=pltpu.VMEM),
        compiler_params=pltpu.CompilerParams(vmem_limit_bytes=16 << 20),
    )(own, other)


def blocks_of(length):
    return (length + (BLOCK - 1)) // BLOCK


def roll_kernel(
    after_ref, x_hbm, g_hbm, bx_hbm, bg_hbm, len_hbm, z_ref,
    x, g, bx, bg, lens, x_sems, g_sems, basis_sems, len_sem,
):
    rolls, span, _ = x_hbm.shape
    per_tile = TILE // BLOCK
    len_copy = pltpu.make_async_copy(len_hbm, lens, len_sem)
    len_copy.start()
    basis_copies = (
        pltpu.make_async_copy(bx_hbm, bx, basis_sems.at[0]),
        pltpu.make_async_copy(bg_hbm, bg, basis_sems.at[1]),
    )

    def copies(roll, block, slot):
        src = pl.ds(pl.multiple_of(block * BLOCK, BLOCK), BLOCK)
        dst = pl.ds(pl.multiple_of(slot * BLOCK, BLOCK), BLOCK)
        return (
            pltpu.make_async_copy(x_hbm.at[roll, src], x.at[dst], x_sems.at[slot]),
            pltpu.make_async_copy(g_hbm.at[roll, src], g.at[dst], g_sems.at[slot]),
        )

    def begin(roll, block, slot):
        for copy in copies(roll, block, slot):
            copy.start()

    for copy in basis_copies:
        copy.start()
    for roll in range(rolls):
        begin(roll, 0, roll)
    len_copy.wait()
    filled = jnp.int32(rolls)
    for roll in range(rolls):
        count = blocks_of(lens[roll])
        shift = filled - 1

        @pl.loop(1, count)
        def _(block):
            begin(roll, block, shift + block)

        filled = filled + count - 1
    for copy in basis_copies:
        copy.wait()

    @pl.loop(0, (filled + (per_tile - 1)) // per_tile)
    def _(tile):
        @pl.loop(tile * per_tile, jnp.minimum(filled, (tile + 1) * per_tile))
        def _(slot):
            for copy in copies(0, 0, slot):
                copy.wait()

        rows = pl.ds(pl.multiple_of(tile * TILE, TILE), TILE)
        sums = []
        for src, basis in ((g, bg), (x, bx)):
            total = None
            for at, step in columns(basis.shape[1]):
                cut = pl.ds(at, step)
                term = times_basis(src[rows, cut], basis[:, cut])
                total = term if total is None else total + term
            sums.append(total)
        z_ref[rows, :] = jnp.concatenate(sums, axis=1)


def project_rolls(after, x, g, bx, bg, lengths):
    rolls, span, wide_x = x.shape
    wide_g = g.shape[2]
    rows = rolls * span
    return pl.pallas_call(
        roll_kernel,
        out_shape=jax.ShapeDtypeStruct((rows, bx.shape[0] + bg.shape[0]), jnp.float32),
        in_specs=[pl.BlockSpec(memory_space=pltpu.HBM)] * 6,
        out_specs=pl.BlockSpec(memory_space=pltpu.VMEM),
        scratch_shapes=[
            pltpu.VMEM((rows, wide_x), x.dtype),
            pltpu.VMEM((rows, wide_g), g.dtype),
            pltpu.VMEM(bx.shape, bx.dtype),
            pltpu.VMEM(bg.shape, bg.dtype),
            pltpu.SMEM(lengths.shape, jnp.int32),
            pltpu.SemaphoreType.DMA((rows // BLOCK,)),
            pltpu.SemaphoreType.DMA((rows // BLOCK,)),
            pltpu.SemaphoreType.DMA((2,)),
            pltpu.SemaphoreType.DMA,
        ],
        compiler_params=pltpu.CompilerParams(vmem_limit_bytes=ROOM),
        cost_estimate=pl.CostEstimate(
            flops=2 * rows * (wide_x + wide_g) * 64, bytes_accessed=12 << 20, transcendentals=0
        ),
    )(after, x, g, bx, bg, lengths)


def units_kernel(lens, own_ref, other_ref, unit_ref):
    rolls = lens.shape[0]
    span = own_ref.shape[0] // rolls
    rest = span - BLOCK
    at = jnp.int32(rolls * BLOCK)
    for roll in range(rolls):
        length = lens[roll]
        head = pl.ds(roll * BLOCK, BLOCK)
        tail = pl.ds(pl.multiple_of(at, BLOCK), rest)
        z = jnp.concatenate(
            [own_ref[head, :] + other_ref[head, :], own_ref[tail, :] + other_ref[tail, :]], axis=0
        )
        keep = lax.broadcasted_iota(jnp.int32, z.shape, 0) < length
        sketch = sketch_of(jnp.where(keep, z, 0.0))
        square = jnp.sum(sketch * sketch, axis=(0, 1), keepdims=True)
        size = sketch.shape[0] * sketch.shape[1]
        unit_ref[roll] = sketch / (jnp.sqrt(square / size + 1e-6) * math.sqrt(size))
        at = at + (blocks_of(length) - 1) * BLOCK


def roll_units(lengths, own, other):
    rolls = lengths.shape[0]
    half = own.shape[1] // 2
    return pl.pallas_call(
        units_kernel,
        out_shape=jax.ShapeDtypeStruct((rolls, half // 2, half * 2), jnp.float32),
        in_specs=[pl.BlockSpec(memory_space=pltpu.SMEM)]
        + [pl.BlockSpec(memory_space=pltpu.VMEM)] * 2,
        out_specs=pl.BlockSpec(memory_space=pltpu.VMEM),
        compiler_params=pltpu.CompilerParams(vmem_limit_bytes=16 << 20),
    )(lengths, own, other)


def score_kernel(order, dp_axis, unit_ref, *refs):
    sketch_refs, out_ref = refs[:-1], refs[-1]
    rolls = unit_ref.shape[0]
    total = len(order)
    me = lax.axis_index(dp_axis)
    lanes = unit_ref.shape[2]
    place = lax.broadcasted_iota(jnp.int32, (total, lanes), 0)
    tables = [jnp.zeros((total, lanes), jnp.float32) for _ in range(rolls + 1)]
    size = unit_ref.shape[1] * lanes
    at = 0
    for ref in sketch_refs:
        for i in range(ref.shape[0]):
            sketch = ref[i]
            here = place == jnp.bitwise_xor(me, order[at])
            for k in range(rolls + 1):
                other = unit_ref[k] if k < rolls else sketch
                row = jnp.sum(sketch * other, axis=0, keepdims=True)
                tables[k] = jnp.where(here, row, tables[k])
            at += 1
    ones = jnp.ones((8, lanes), jnp.float32)
    added = [
        lax.dot_general(
            ones, table, (((1,), (1,)), ((), ())),
            preferred_element_type=jnp.float32, precision=EXACT,
        )
        for table in tables
    ]
    spread = jnp.sqrt(added[rolls] / size + 1e-6)
    out_ref[...] = jnp.concatenate([(added[k] / spread)[0:1] for k in range(rolls)], axis=0)


def score(units, sketches, order):
    return pl.pallas_call(
        functools.partial(score_kernel, order, "dp"),
        out_shape=jax.ShapeDtypeStruct((units.shape[0], len(order)), jnp.float32),
        in_specs=[pl.BlockSpec(memory_space=pltpu.VMEM)] * (1 + len(sketches)),
        out_specs=pl.BlockSpec(memory_space=pltpu.VMEM),
        compiler_params=pltpu.CompilerParams(vmem_limit_bytes=16 << 20),
    )(units, *sketches)


def other_core(value):
    return lax.ppermute(value, "tensor", [(0, 1), (1, 0)])


def on_device(
    devices, roll_inputs, roll_grads, ref_inputs, ref_grads, in_basis, out_basis,
    roll_lengths, ref_lengths,
):
    bx, bg = in_basis.T, out_basis.T
    ref_z = project_ref(ref_inputs, ref_grads, bx, bg, ref_lengths)
    sketch = ref_sketch(ref_z, other_core(ref_z))
    roll_z = project_rolls(sketch, roll_inputs, roll_grads, bx, bg, roll_lengths)

    held = sketch[None]
    order = [0]
    bits = [1 << k for k in range(devices.bit_length() - 1)][::-1]
    for step, bit in enumerate(bits):
        got = lax.ppermute(held, "dp", [(i, i ^ bit) for i in range(devices)])
        if step == 0:
            got, roll_z = lax.optimization_barrier((got, roll_z))
            units = roll_units(roll_lengths, roll_z, other_core(roll_z))
        order = order + [k ^ bit for k in order]
        if step < len(bits) - 1:
            held = jnp.concatenate([held, got], axis=0)
    return score(units, (held, got), tuple(order))


def solution(mesh):
    placed = (
        P(("group", "dp"), None, "tensor"),
        P(("group", "dp"), None, "tensor"),
        P(("group", "dp"), None, "tensor"),
        P(("group", "dp"), None, "tensor"),
        P("tensor", None),
        P("tensor", None),
        P(("group", "dp")),
        P(("group", "dp")),
    )
    return jax.shard_map(
        functools.partial(on_device, mesh.shape["dp"]),
        mesh=mesh,
        in_specs=placed,
        out_specs=P(("group", "dp"), None),
        check_vma=False,
    )
```

```python
import functools
import math

import jax
import jax.numpy as jnp
from jax import lax
from jax.experimental import pallas as pl
from jax.experimental.pallas import tpu as pltpu
from jax.sharding import PartitionSpec as P

STEP = 16
TILE = 32
REF_ROOM = 8 << 20
ROLL_ROOM = 8 << 20
EXACT = lax.Precision.HIGHEST


def columns(width):
    step = 1024 if width % 1024 == 0 else width
    return [(at, step) for at in range(0, width, step)]


def times_basis(rows, basis):
    return lax.dot_general(
        rows, basis, (((1,), (1,)), ((), ())), preferred_element_type=jnp.float32
    )


def ref_kernel(x_hbm, g_hbm, bx_hbm, bg_hbm, z_ref, bg, x, g, bx, sems):
    work = []
    for part, (src, basis_src, dst, basis_dst) in enumerate(
        ((x_hbm, bx_hbm, x, bx), (g_hbm, bg_hbm, g, bg))
    ):
        for at, step in columns(src.shape[2]):
            cut = pl.ds(at, step)
            k = len(work)
            copies = (
                pltpu.make_async_copy(basis_src.at[:, cut], basis_dst.at[:, cut], sems.at[0, k]),
                pltpu.make_async_copy(src.at[0, :, cut], dst.at[:, cut], sems.at[1, k]),
            )
            for copy in copies:
                copy.start()
            work.append((part, dst, basis_dst, cut, copies))
    sums = [None, None]
    for part, rows, basis, cut, copies in work:
        for copy in copies:
            copy.wait()
        term = times_basis(rows[:, cut], basis[:, cut])
        sums[part] = term if sums[part] is None else sums[part] + term
    z_ref[...] = jnp.concatenate([sums[1], sums[0]], axis=1)


def project_ref(x, g, bx, bg):
    span, wide_x, wide_g = x.shape[1], x.shape[2], g.shape[2]
    parts = len(columns(wide_x)) + len(columns(wide_g))
    return pl.pallas_call(
        ref_kernel,
        out_shape=(
            jax.ShapeDtypeStruct((span, bx.shape[0] + bg.shape[0]), jnp.float32),
            jax.ShapeDtypeStruct(bg.shape, bg.dtype),
        ),
        in_specs=[pl.BlockSpec(memory_space=pl.ANY)] * 4,
        out_specs=(pl.BlockSpec(memory_space=pltpu.VMEM),) * 2,
        scratch_shapes=[
            pltpu.VMEM((span, wide_x), x.dtype),
            pltpu.VMEM((span, wide_g), g.dtype),
            pltpu.VMEM(bx.shape, bx.dtype),
            pltpu.SemaphoreType.DMA((2, parts)),
        ],
        compiler_params=pltpu.CompilerParams(vmem_limit_bytes=REF_ROOM),
        cost_estimate=pl.CostEstimate(flops=20_000_000_000, bytes_accessed=60 << 20, transcendentals=0),
    )(*(pltpu.with_memory_space_constraint(a, pltpu.HBM) for a in (x, g, bx, bg)))


def sketch_of(z):
    half = z.shape[1] // 2
    full = lax.dot_general(
        z[:, :half], z[:, half:], (((0,), (0,)), ((), ())),
        preferred_element_type=jnp.float32, precision=EXACT,
    )
    rows = half // 2
    return jnp.concatenate([full[:rows], full[rows:]], axis=1)


def sketch_kernel(len_ref, own_ref, other_ref, sketch_ref):
    z = own_ref[...] + other_ref[...]
    keep = lax.broadcasted_iota(jnp.int32, z.shape, 0) < len_ref[...]
    sketch_ref[...] = sketch_of(jnp.where(keep, z, 0.0))


def ref_sketch(length, own, other):
    half = own.shape[1] // 2
    return pl.pallas_call(
        sketch_kernel,
        out_shape=jax.ShapeDtypeStruct((half // 2, half * 2), jnp.float32),
        in_specs=[pl.BlockSpec(memory_space=pltpu.VMEM)] * 3,
        out_specs=pl.BlockSpec(memory_space=pltpu.VMEM),
        compiler_params=pltpu.CompilerParams(vmem_limit_bytes=8 << 20),
    )(length, own, other)


def by_length(lens, rolls):
    ranks = []
    for i in range(rolls):
        rank = jnp.int32(0)
        for j in range(rolls):
            if j != i:
                ahead = lens[j] >= lens[i] if j < i else lens[j] > lens[i]
                rank = rank + ahead.astype(jnp.int32)
        ranks.append(rank)
    return [
        sum(jnp.where(ranks[i] == place, jnp.int32(i), 0) for i in range(rolls))
        for place in range(rolls)
    ], ranks


def steps_of(length):
    return (length + (STEP - 1)) // STEP


def roll_kernel(places, after_ref, lens, x_ref, g_ref, bx_ref, bg_ref, z_ref):
    rolls, span, _ = x_ref.shape
    numbers, _ = by_length(lens, rolls)
    half = bg_ref.shape[0]

    @pl.loop(0, len(places))
    def _(slot):
        roll = sum(jnp.where(slot == k, numbers[p], 0) for k, p in enumerate(places))
        need = (lens[roll] + (TILE - 1)) // TILE
        for tiles in range(1, span // TILE + 1):

            @pl.when(need == tiles)
            def _():
                rows = pl.ds(0, tiles * TILE)
                for k, (src, basis) in enumerate(((g_ref, bg_ref), (x_ref, bx_ref))):
                    z_ref[slot, rows, k * half : (k + 1) * half] = times_basis(
                        src[roll, rows, :], basis[...]
                    )


def project_rolls(places, after, x, g, bx, bg, lengths):
    rolls, span, wide_x = x.shape
    wide_g = g.shape[2]
    count = len(places)
    held = pl.BlockSpec(memory_space=pltpu.VMEM)
    return pl.pallas_call(
        functools.partial(roll_kernel, places),
        out_shape=jax.ShapeDtypeStruct((count, span, bx.shape[0] * 2), jnp.float32),
        in_specs=[
            pl.BlockSpec(memory_space=pl.ANY),
            pl.BlockSpec(memory_space=pltpu.SMEM),
            held, held, held, held,
        ],
        out_specs=held,
        compiler_params=pltpu.CompilerParams(vmem_limit_bytes=ROLL_ROOM),
        cost_estimate=pl.CostEstimate(
            flops=2 * count * span * (wide_x + wide_g) * 64,
            bytes_accessed=6 << 20,
            transcendentals=0,
        ),
    )(after, lengths, x, g, bx, bg)


def units_kernel(shares, lens, *refs):
    unit_ref = refs[-1]
    rolls = lens.shape[0]
    _, ranks = by_length(lens, rolls)
    span = refs[0].shape[1]
    for share, places in enumerate(shares):
        own_ref, other_ref = refs[2 * share : 2 * share + 2]
        for slot, place in enumerate(places):
            roll = sum(jnp.where(ranks[i] == place, jnp.int32(i), 0) for i in range(rolls))
            z = own_ref[slot] + other_ref[slot]
            keep = lax.broadcasted_iota(jnp.int32, z.shape, 0) < lens[roll]
            sketch = sketch_of(jnp.where(keep, z, 0.0))
            square = jnp.sum(sketch * sketch, axis=(0, 1), keepdims=True)
            size = sketch.shape[0] * sketch.shape[1]
            unit_ref[roll] = sketch / (jnp.sqrt(square / size + 1e-6) * math.sqrt(size))


def roll_units(shares, lengths, parts):
    rolls = lengths.shape[0]
    half = parts[0][0].shape[2] // 2
    flat = [z for pair in parts for z in pair]
    return pl.pallas_call(
        functools.partial(units_kernel, shares),
        out_shape=jax.ShapeDtypeStruct((rolls, half // 2, half * 2), jnp.float32),
        in_specs=[pl.BlockSpec(memory_space=pltpu.SMEM)]
        + [pl.BlockSpec(memory_space=pltpu.VMEM)] * len(flat),
        out_specs=pl.BlockSpec(memory_space=pltpu.VMEM),
        compiler_params=pltpu.CompilerParams(vmem_limit_bytes=8 << 20),
    )(lengths, *flat)


def score_kernel(order, dp_axis, unit_ref, *refs):
    sketch_refs, out_ref = refs[:-1], refs[-1]
    rolls = unit_ref.shape[0]
    total = len(order)
    me = lax.axis_index(dp_axis)
    lanes = unit_ref.shape[2]
    place = lax.broadcasted_iota(jnp.int32, (total, lanes), 0)
    tables = [jnp.zeros((total, lanes), jnp.float32) for _ in range(rolls + 1)]
    size = unit_ref.shape[1] * lanes
    at = 0
    for ref in sketch_refs:
        for i in range(ref.shape[0]):
            sketch = ref[i]
            here = place == jnp.bitwise_xor(me, order[at])
            for k in range(rolls + 1):
                other = unit_ref[k] if k < rolls else sketch
                row = jnp.sum(sketch * other, axis=0, keepdims=True)
                tables[k] = jnp.where(here, row, tables[k])
            at += 1
    ones = jnp.ones((8, lanes), jnp.float32)
    added = [
        lax.dot_general(
            ones, table, (((1,), (1,)), ((), ())),
            preferred_element_type=jnp.float32, precision=EXACT,
        )
        for table in tables
    ]
    spread = jnp.sqrt(added[rolls] / size + 1e-6)
    out_ref[...] = jnp.concatenate([(added[k] / spread)[0:1] for k in range(rolls)], axis=0)


def score(units, sketches, order):
    return pl.pallas_call(
        functools.partial(score_kernel, order, "dp"),
        out_shape=jax.ShapeDtypeStruct((units.shape[0], len(order)), jnp.float32),
        in_specs=[pl.BlockSpec(memory_space=pltpu.VMEM)] * (1 + len(sketches)),
        out_specs=pl.BlockSpec(memory_space=pltpu.VMEM),
        compiler_params=pltpu.CompilerParams(vmem_limit_bytes=8 << 20),
    )(units, *sketches)


def other_core(value):
    return lax.ppermute(value, "tensor", [(0, 1), (1, 0)])


def on_device(
    devices, roll_inputs, roll_grads, ref_inputs, ref_grads, in_basis, out_basis,
    roll_lengths, ref_lengths,
):
    bx, bg = in_basis.T, out_basis.T
    shares = ((0, 3), (1, 2))
    ref_z, bg = project_ref(ref_inputs, ref_grads, bx, bg)
    sketch = ref_sketch(ref_lengths[None], ref_z, other_core(ref_z))

    held = sketch[None]
    order = [0]
    bits = [1 << k for k in range(devices.bit_length() - 1)][::-1]
    parts = []
    for step, bit in enumerate(bits):
        got = lax.ppermute(held, "dp", [(i, i ^ bit) for i in range(devices)])
        if step < len(shares):
            z = project_rolls(shares[step], held, roll_inputs, roll_grads, bx, bg, roll_lengths)
            got, z = lax.optimization_barrier((got, z))
            parts.append((z, other_core(z)))
        order = order + [k ^ bit for k in order]
        if step < len(bits) - 1:
            held = jnp.concatenate([held, got], axis=0)
    units = roll_units(shares, roll_lengths, parts)
    return score(units, (held, got), tuple(order))


def solution(mesh):
    placed = (
        P(("group", "dp"), None, "tensor"),
        P(("group", "dp"), None, "tensor"),
        P(("group", "dp"), None, "tensor"),
        P(("group", "dp"), None, "tensor"),
        P("tensor", None),
        P("tensor", None),
        P(("group", "dp")),
        P(("group", "dp")),
    )
    return jax.shard_map(
        functools.partial(on_device, mesh.shape["dp"]),
        mesh=mesh,
        in_specs=placed,
        out_specs=P(("group", "dp"), None),
        check_vma=False,
    )
```

```python
import functools
import math

import jax
import jax.numpy as jnp
from jax import lax
from jax.experimental import pallas as pl
from jax.experimental.pallas import tpu as pltpu
from jax.sharding import PartitionSpec as P

CHUNK = 2048
TILE = 32
REF_ROOM = 8 << 20
ROLL_ROOM = 8 << 20
EXACT = lax.Precision.HIGHEST


def columns(width):
    return [(at, min(CHUNK, width - at)) for at in range(0, width, CHUNK)]


def times_basis(rows, basis):
    return lax.dot_general(
        rows, basis, (((1,), (1,)), ((), ())), preferred_element_type=jnp.float32
    )


def ref_kernel(x_hbm, g_hbm, bx_hbm, bg_hbm, z_ref, bx, bg, x, g, sems):
    work = []
    for part, (src, basis_src, dst, basis_dst) in enumerate(
        ((x_hbm, bx_hbm, x, bx), (g_hbm, bg_hbm, g, bg))
    ):
        for at, step in columns(src.shape[2]):
            cut = pl.ds(at, step)
            k = len(work)
            copies = (
                pltpu.make_async_copy(basis_src.at[:, cut], basis_dst.at[:, cut], sems.at[0, k]),
                pltpu.make_async_copy(src.at[0, :, cut], dst.at[:, cut], sems.at[1, k]),
            )
            for copy in copies:
                copy.start()
            work.append((part, dst, basis_dst, cut, copies))
    sums = [None, None]
    for part, rows, basis, cut, copies in work:
        for copy in copies:
            copy.wait()
        term = times_basis(rows[:, cut], basis[:, cut])
        sums[part] = term if sums[part] is None else sums[part] + term
    z_ref[...] = jnp.concatenate([sums[1], sums[0]], axis=1)


def project_ref(x, g, bx, bg):
    span, wide_x, wide_g = x.shape[1], x.shape[2], g.shape[2]
    parts = len(columns(wide_x)) + len(columns(wide_g))
    return pl.pallas_call(
        ref_kernel,
        out_shape=(
            jax.ShapeDtypeStruct((span, bx.shape[0] + bg.shape[0]), jnp.float32),
            jax.ShapeDtypeStruct(bx.shape, bx.dtype),
            jax.ShapeDtypeStruct(bg.shape, bg.dtype),
        ),
        in_specs=[pl.BlockSpec(memory_space=pl.ANY)] * 4,
        out_specs=(pl.BlockSpec(memory_space=pltpu.VMEM),) * 3,
        scratch_shapes=[
            pltpu.VMEM((span, wide_x), x.dtype),
            pltpu.VMEM((span, wide_g), g.dtype),
            pltpu.SemaphoreType.DMA((2, parts)),
        ],
        compiler_params=pltpu.CompilerParams(vmem_limit_bytes=REF_ROOM),
        cost_estimate=pl.CostEstimate(flops=20_000_000_000, bytes_accessed=60 << 20, transcendentals=0),
    )(*(pltpu.with_memory_space_constraint(a, pltpu.HBM) for a in (x, g, bx, bg)))


def sketch_of(z):
    half = z.shape[1] // 2
    full = lax.dot_general(
        z[:, :half], z[:, half:], (((0,), (0,)), ((), ())),
        preferred_element_type=jnp.float32, precision=EXACT,
    )
    rows = half // 2
    return jnp.concatenate([full[:rows], full[rows:]], axis=1)


def sketch_kernel(len_ref, own_ref, other_ref, sketch_ref):
    z = own_ref[...] + other_ref[...]
    keep = lax.broadcasted_iota(jnp.int32, z.shape, 0) < len_ref[0]
    sketch_ref[...] = sketch_of(jnp.where(keep, z, 0.0))


def ref_sketch(length, own, other):
    half = own.shape[1] // 2
    return pl.pallas_call(
        sketch_kernel,
        out_shape=jax.ShapeDtypeStruct((half // 2, half * 2), jnp.float32),
        in_specs=[pl.BlockSpec(memory_space=pltpu.SMEM)]
        + [pl.BlockSpec(memory_space=pltpu.VMEM)] * 2,
        out_specs=pl.BlockSpec(memory_space=pltpu.VMEM),
        compiler_params=pltpu.CompilerParams(vmem_limit_bytes=8 << 20),
    )(length, own, other)


def by_length(lens, rolls):
    ranks = []
    for i in range(rolls):
        rank = jnp.int32(0)
        for j in range(rolls):
            if j != i:
                ahead = lens[j] >= lens[i] if j < i else lens[j] > lens[i]
                rank = rank + ahead.astype(jnp.int32)
        ranks.append(rank)
    return [
        sum(jnp.where(ranks[i] == place, jnp.int32(i), 0) for i in range(rolls))
        for place in range(rolls)
    ], ranks


def steps_of(length):
    return (length + (STEP - 1)) // STEP


def roll_kernel(places, after_ref, lens, x_ref, g_ref, bx_ref, bg_ref, z_ref):
    rolls, span, _ = x_ref.shape
    numbers, _ = by_length(lens, rolls)
    half = bg_ref.shape[0]

    @pl.loop(0, len(places))
    def _(slot):
        roll = sum(jnp.where(slot == k, numbers[p], 0) for k, p in enumerate(places))
        need = (lens[roll] + (TILE - 1)) // TILE
        for tiles in range(1, span // TILE + 1):

            @pl.when(need == tiles)
            def _():
                rows = pl.ds(0, tiles * TILE)
                for k, (src, basis) in enumerate(((g_ref, bg_ref), (x_ref, bx_ref))):
                    z_ref[slot, rows, k * half : (k + 1) * half] = times_basis(
                        src[roll, rows, :], basis[...]
                    )


def project_rolls(places, after, x, g, bx, bg, lengths):
    rolls, span, wide_x = x.shape
    wide_g = g.shape[2]
    count = len(places)
    held = pl.BlockSpec(memory_space=pltpu.VMEM)
    return pl.pallas_call(
        functools.partial(roll_kernel, places),
        out_shape=jax.ShapeDtypeStruct((count, span, bx.shape[0] * 2), jnp.float32),
        in_specs=[
            pl.BlockSpec(memory_space=pl.ANY),
            pl.BlockSpec(memory_space=pltpu.SMEM),
            held, held, held, held,
        ],
        out_specs=held,
        compiler_params=pltpu.CompilerParams(vmem_limit_bytes=ROLL_ROOM),
        cost_estimate=pl.CostEstimate(
            flops=2 * count * span * (wide_x + wide_g) * 64,
            bytes_accessed=6 << 20,
            transcendentals=0,
        ),
    )(after, lengths, x, g, bx, bg)


def units_kernel(shares, lens, *refs):
    unit_ref = refs[-1]
    rolls = lens.shape[0]
    _, ranks = by_length(lens, rolls)
    span = refs[0].shape[1]
    for share, places in enumerate(shares):
        own_ref, other_ref = refs[2 * share : 2 * share + 2]
        for slot, place in enumerate(places):
            roll = sum(jnp.where(ranks[i] == place, jnp.int32(i), 0) for i in range(rolls))
            z = own_ref[slot] + other_ref[slot]
            keep = lax.broadcasted_iota(jnp.int32, z.shape, 0) < lens[roll]
            sketch = sketch_of(jnp.where(keep, z, 0.0))
            square = jnp.sum(sketch * sketch, axis=(0, 1), keepdims=True)
            size = sketch.shape[0] * sketch.shape[1]
            unit_ref[roll] = sketch / (jnp.sqrt(square / size + 1e-6) * math.sqrt(size))


def roll_units(shares, lengths, parts):
    rolls = lengths.shape[0]
    half = parts[0][0].shape[2] // 2
    flat = [z for pair in parts for z in pair]
    return pl.pallas_call(
        functools.partial(units_kernel, shares),
        out_shape=jax.ShapeDtypeStruct((rolls, half // 2, half * 2), jnp.float32),
        in_specs=[pl.BlockSpec(memory_space=pltpu.SMEM)]
        + [pl.BlockSpec(memory_space=pltpu.VMEM)] * len(flat),
        out_specs=pl.BlockSpec(memory_space=pltpu.VMEM),
        compiler_params=pltpu.CompilerParams(vmem_limit_bytes=8 << 20),
    )(lengths, *flat)


def score_kernel(order, dp_axis, unit_ref, *refs):
    sketch_refs, out_ref = refs[:-1], refs[-1]
    rolls = unit_ref.shape[0]
    total = len(order)
    me = lax.axis_index(dp_axis)
    lanes = unit_ref.shape[2]
    place = lax.broadcasted_iota(jnp.int32, (total, lanes), 0)
    tables = [jnp.zeros((total, lanes), jnp.float32) for _ in range(rolls + 1)]
    size = unit_ref.shape[1] * lanes
    at = 0
    for ref in sketch_refs:
        for i in range(ref.shape[0]):
            sketch = ref[i]
            here = place == jnp.bitwise_xor(me, order[at])
            for k in range(rolls + 1):
                other = unit_ref[k] if k < rolls else sketch
                row = jnp.sum(sketch * other, axis=0, keepdims=True)
                tables[k] = jnp.where(here, row, tables[k])
            at += 1
    ones = jnp.ones((8, lanes), jnp.float32)
    added = [
        lax.dot_general(
            ones, table, (((1,), (1,)), ((), ())),
            preferred_element_type=jnp.float32, precision=EXACT,
        )
        for table in tables
    ]
    spread = jnp.sqrt(added[rolls] / size + 1e-6)
    out_ref[...] = jnp.concatenate([(added[k] / spread)[0:1] for k in range(rolls)], axis=0)


def score(units, sketches, order):
    return pl.pallas_call(
        functools.partial(score_kernel, order, "dp"),
        out_shape=jax.ShapeDtypeStruct((units.shape[0], len(order)), jnp.float32),
        in_specs=[pl.BlockSpec(memory_space=pltpu.VMEM)] * (1 + len(sketches)),
        out_specs=pl.BlockSpec(memory_space=pltpu.VMEM),
        compiler_params=pltpu.CompilerParams(vmem_limit_bytes=8 << 20),
    )(units, *sketches)


def other_core(value):
    return lax.ppermute(value, "tensor", [(0, 1), (1, 0)])


def from_chip(value, bit, devices, cores):
    pairs = [
        (i * cores + t, (i ^ bit) * cores + (t + 1) % cores)
        for i in range(devices)
        for t in range(cores)
    ]
    return lax.ppermute(value, ("dp", "tensor"), pairs)


def on_device(
    devices, cores, roll_inputs, roll_grads, ref_inputs, ref_grads, in_basis, out_basis,
    roll_lengths, ref_lengths,
):
    bx, bg = in_basis.T, out_basis.T
    shares = ((0, 3), (1, 2))
    ref_z, bx, bg = project_ref(ref_inputs, ref_grads, bx, bg)
    sketch = ref_sketch(ref_lengths, ref_z, other_core(ref_z))

    held = sketch[None]
    order = [0]
    bits = [1 << k for k in range(devices.bit_length() - 1)][::-1]
    parts = []
    for step, bit in enumerate(bits):
        got = from_chip(held, bit, devices, cores)
        if step < len(shares):
            z = project_rolls(shares[step], held, roll_inputs, roll_grads, bx, bg, roll_lengths)
            got, z = lax.optimization_barrier((got, z))
            parts.append((z, other_core(z)))
        order = order + [k ^ bit for k in order]
        if step < len(bits) - 1:
            held = jnp.concatenate([held, got], axis=0)
    units = roll_units(shares, roll_lengths, parts)
    return score(units, (held, got), tuple(order))


def solution(mesh):
    placed = (
        P(("group", "dp"), None, "tensor"),
        P(("group", "dp"), None, "tensor"),
        P(("group", "dp"), None, "tensor"),
        P(("group", "dp"), None, "tensor"),
        P("tensor", None),
        P("tensor", None),
        P(("group", "dp")),
        P(("group", "dp")),
    )
    return jax.shard_map(
        functools.partial(on_device, mesh.shape["dp"], mesh.shape["tensor"]),
        mesh=mesh,
        in_specs=placed,
        out_specs=P(("group", "dp"), None),
        check_vma=False,
    )
```

```python
import functools
import math

import jax
import jax.numpy as jnp
from jax import lax
from jax.experimental import pallas as pl
from jax.experimental.pallas import tpu as pltpu
from jax.sharding import PartitionSpec as P

CHUNK = 2048
TILE = 32
REF_ROOM = 51_000_000
ROLL_ROOM = 8 << 20
EXACT = lax.Precision.HIGHEST


def columns(width):
    return [(at, min(CHUNK, width - at)) for at in range(0, width, CHUNK)]


def times_basis(rows, basis):
    return lax.dot_general(
        rows, basis, (((1,), (1,)), ((), ())), preferred_element_type=jnp.float32
    )


def ref_kernel(x_hbm, g_hbm, bx_hbm, bg_hbm, z_ref, bx, bg, x, g, sems):
    work = []
    for part, (src, basis_src, dst, basis_dst) in enumerate(
        ((x_hbm, bx_hbm, x, bx), (g_hbm, bg_hbm, g, bg))
    ):
        for at, step in columns(src.shape[2]):
            cut = pl.ds(at, step)
            k = len(work)
            copies = (
                pltpu.make_async_copy(basis_src.at[:, cut], basis_dst.at[:, cut], sems.at[0, k]),
                pltpu.make_async_copy(src.at[0, :, cut], dst.at[:, cut], sems.at[1, k]),
            )
            for copy in copies:
                copy.start()
            work.append((part, dst, basis_dst, cut, copies))
    sums = [None, None]
    for part, rows, basis, cut, copies in work:
        for copy in copies:
            copy.wait()
        term = times_basis(rows[:, cut], basis[:, cut])
        sums[part] = term if sums[part] is None else sums[part] + term
    z_ref[...] = jnp.concatenate([sums[1], sums[0]], axis=1)


def project_ref(x, g, bx, bg):
    span, wide_x, wide_g = x.shape[1], x.shape[2], g.shape[2]
    parts = len(columns(wide_x)) + len(columns(wide_g))
    return pl.pallas_call(
        ref_kernel,
        out_shape=(
            jax.ShapeDtypeStruct((span, bx.shape[0] + bg.shape[0]), jnp.float32),
            jax.ShapeDtypeStruct(bx.shape, bx.dtype),
            jax.ShapeDtypeStruct(bg.shape, bg.dtype),
        ),
        in_specs=[pl.BlockSpec(memory_space=pl.ANY)] * 4,
        out_specs=(pl.BlockSpec(memory_space=pltpu.VMEM),) * 3,
        scratch_shapes=[
            pltpu.VMEM((span, wide_x), x.dtype),
            pltpu.VMEM((span, wide_g), g.dtype),
            pltpu.SemaphoreType.DMA((2, parts)),
        ],
        compiler_params=pltpu.CompilerParams(vmem_limit_bytes=REF_ROOM),
        cost_estimate=pl.CostEstimate(flops=20000000000, bytes_accessed=62914560, transcendentals=0),
    )(*(pltpu.with_memory_space_constraint(a, pltpu.HBM) for a in (x, g, bx, bg)))


def sketch_of(z):
    half = z.shape[1] // 2
    full = lax.dot_general(
        z[:, :half], z[:, half:], (((0,), (0,)), ((), ())),
        preferred_element_type=jnp.float32, precision=EXACT,
    )
    rows = half // 2
    return jnp.concatenate([full[:rows], full[rows:]], axis=1)


def sketch_kernel(len_ref, own_ref, other_ref, sketch_ref):
    z = own_ref[...] + other_ref[...]
    keep = lax.broadcasted_iota(jnp.int32, z.shape, 0) < len_ref[0]
    sketch_ref[...] = sketch_of(jnp.where(keep, z, 0.0))


def ref_sketch(length, own, other):
    half = own.shape[1] // 2
    return pl.pallas_call(
        sketch_kernel,
        out_shape=jax.ShapeDtypeStruct((half // 2, half * 2), jnp.float32),
        in_specs=[pl.BlockSpec(memory_space=pltpu.SMEM)]
        + [pl.BlockSpec(memory_space=pltpu.VMEM)] * 2,
        out_specs=pl.BlockSpec(memory_space=pltpu.VMEM),
        compiler_params=pltpu.CompilerParams(vmem_limit_bytes=8 << 20),
        cost_estimate=pl.CostEstimate(flops=2000000000, bytes_accessed=6291456, transcendentals=0),
    )(length, own, other)


def by_length(lens, rolls):
    ranks = []
    for i in range(rolls):
        rank = jnp.int32(0)
        for j in range(rolls):
            if j != i:
                ahead = lens[j] >= lens[i] if j < i else lens[j] > lens[i]
                rank = rank + ahead.astype(jnp.int32)
        ranks.append(rank)
    return [
        sum(jnp.where(ranks[i] == place, jnp.int32(i), 0) for i in range(rolls))
        for place in range(rolls)
    ]


def roll_kernel(places, earlier, *refs):
    _, lens, x_ref, g_ref, bx_ref, bg_ref, z_ref = refs[earlier:]
    rolls, span, _ = x_ref.shape
    row = lens[...]
    lens = [row[i] for i in range(rolls)]
    numbers = by_length(lens, rolls)
    half = bg_ref.shape[0]

    @pl.loop(0, len(places))
    def _(slot):
        roll = sum(jnp.where(slot == k, numbers[p], 0) for k, p in enumerate(places))
        need = (sum(jnp.where(roll == i, lens[i], 0) for i in range(rolls)) + (TILE - 1)) // TILE
        for tiles in range(1, span // TILE + 1):

            @pl.when(need == tiles)
            def _():
                rows = pl.ds(0, tiles * TILE)
                for k, (src, basis) in enumerate(((g_ref, bg_ref), (x_ref, bx_ref))):
                    z_ref[roll, rows, k * half : (k + 1) * half] = times_basis(
                        src[roll, rows, :], basis[...]
                    )


def project_rolls(places, earlier, after, x, g, bx, bg, lengths):
    rolls, span, wide_x = x.shape
    held = pl.BlockSpec(memory_space=pltpu.VMEM)
    outside = pl.BlockSpec(memory_space=pl.ANY)
    return pl.pallas_call(
        functools.partial(roll_kernel, places, len(earlier)),
        out_shape=jax.ShapeDtypeStruct((rolls, span, bx.shape[0] * 2), jnp.float32),
        in_specs=[held] * len(earlier)
        + [outside, held, held, held, held, held],
        out_specs=held,
        input_output_aliases={0: 0} if earlier else {},
        compiler_params=pltpu.CompilerParams(vmem_limit_bytes=ROLL_ROOM),
        cost_estimate=pl.CostEstimate(
            flops=2 * len(places) * span * (wide_x + g.shape[2]) * 64,
            bytes_accessed=6 << 20,
            transcendentals=0,
        ),
    )(*earlier, after, lengths, x, g, bx, bg)


def units_kernel(lens, own_ref, other_ref, unit_ref):
    row = lens[...]
    rolls = [row[i] for i in range(lens.shape[0])]
    for roll, length in enumerate(rolls):
        z = own_ref[roll] + other_ref[roll]
        keep = lax.broadcasted_iota(jnp.int32, z.shape, 0) < length
        sketch = sketch_of(jnp.where(keep, z, 0.0))
        square = jnp.sum(sketch * sketch, axis=(0, 1), keepdims=True)
        size = sketch.shape[0] * sketch.shape[1]
        unit_ref[roll] = sketch / (jnp.sqrt(square / size + 1e-6) * math.sqrt(size))


def roll_units(lengths, own, other):
    rolls = lengths.shape[0]
    half = own.shape[2] // 2
    return pl.pallas_call(
        units_kernel,
        out_shape=jax.ShapeDtypeStruct((rolls, half // 2, half * 2), jnp.float32),
        in_specs=[pl.BlockSpec(memory_space=pltpu.VMEM)] * 3,
        out_specs=pl.BlockSpec(memory_space=pltpu.VMEM),
        compiler_params=pltpu.CompilerParams(vmem_limit_bytes=8 << 20),
    )(lengths, own, other)


def score_kernel(order, dp_axis, unit_ref, *refs):
    sketch_refs, out_ref = refs[:-1], refs[-1]
    rolls = unit_ref.shape[0]
    total = len(order)
    me = lax.axis_index(dp_axis)
    lanes = unit_ref.shape[2]
    place = lax.broadcasted_iota(jnp.int32, (total, lanes), 0)
    tables = [jnp.zeros((total, lanes), jnp.float32) for _ in range(rolls + 1)]
    size = unit_ref.shape[1] * lanes
    at = 0
    for ref in sketch_refs:
        for i in range(ref.shape[0]):
            sketch = ref[i]
            here = place == jnp.bitwise_xor(me, order[at])
            for k in range(rolls + 1):
                other = unit_ref[k] if k < rolls else sketch
                row = jnp.sum(sketch * other, axis=0, keepdims=True)
                tables[k] = jnp.where(here, row, tables[k])
            at += 1
    ones = jnp.ones((8, lanes), jnp.float32)
    added = [
        lax.dot_general(
            ones, table, (((1,), (1,)), ((), ())),
            preferred_element_type=jnp.float32, precision=EXACT,
        )
        for table in tables
    ]
    spread = jnp.sqrt(added[rolls] / size + 1e-6)
    out_ref[...] = jnp.concatenate([(added[k] / spread)[0:1] for k in range(rolls)], axis=0)


def score(units, sketches, order):
    return pl.pallas_call(
        functools.partial(score_kernel, order, "dp"),
        out_shape=jax.ShapeDtypeStruct((units.shape[0], len(order)), jnp.float32),
        in_specs=[pl.BlockSpec(memory_space=pltpu.VMEM)] * (1 + len(sketches)),
        out_specs=pl.BlockSpec(memory_space=pltpu.VMEM),
        compiler_params=pltpu.CompilerParams(vmem_limit_bytes=8 << 20),
    )(units, *sketches)


def other_core(value):
    return lax.ppermute(value, "tensor", [(0, 1), (1, 0)])


def from_chip(value, bit, devices, cores):
    pairs = [
        (i * cores + t, (i ^ bit) * cores + (t + 1) % cores)
        for i in range(devices)
        for t in range(cores)
    ]
    return lax.ppermute(value, ("dp", "tensor"), pairs)


def on_device(
    devices, cores, roll_inputs, roll_grads, ref_inputs, ref_grads, in_basis, out_basis,
    roll_lengths, ref_lengths,
):
    bx, bg = in_basis.T, out_basis.T
    shares = ((0, 3), (1, 2))
    ref_z, bx, bg = project_ref(ref_inputs, ref_grads, bx, bg)
    sketch = ref_sketch(ref_lengths, ref_z, other_core(ref_z))

    held = sketch[None]
    order = [0]
    bits = [1 << k for k in range(devices.bit_length() - 1)][::-1]
    roll_z = ()
    for step, bit in enumerate(bits):
        last = step == len(bits) - 1
        if last:
            held, z = lax.optimization_barrier((held, z))
        got = from_chip(held, bit, devices, cores)
        if step < len(shares):
            z = project_rolls(shares[step], roll_z, held, roll_inputs, roll_grads, bx, bg, roll_lengths)
            got, z = lax.optimization_barrier((got, z))
            roll_z = (z,)
        order = order + [k ^ bit for k in order]
        if not last:
            held = jnp.concatenate([held, got], axis=0)
    units = roll_units(roll_lengths, z, other_core(z))
    return score(units, (held, got), tuple(order))


def solution(mesh):
    placed = (
        P(("group", "dp"), None, "tensor"),
        P(("group", "dp"), None, "tensor"),
        P(("group", "dp"), None, "tensor"),
        P(("group", "dp"), None, "tensor"),
        P("tensor", None),
        P("tensor", None),
        P(("group", "dp")),
        P(("group", "dp")),
    )
    return jax.shard_map(
        functools.partial(on_device, mesh.shape["dp"], mesh.shape["tensor"]),
        mesh=mesh,
        in_specs=placed,
        out_specs=P(("group", "dp"), None),
        check_vma=False,
    )
```

```python
import functools
import math

import jax
import jax.numpy as jnp
from jax import lax
from jax.experimental import pallas as pl
from jax.experimental.pallas import tpu as pltpu
from jax.sharding import PartitionSpec as P

CHUNK = 2048
TILE = 32
REF_ROOM = 51_000_000
ROLL_ROOM = 20 << 20
EXACT = lax.Precision.HIGHEST
ROOM_FOR_PREFETCH = pl.CostEstimate(
    flops=20_000_000_000, bytes_accessed=60 << 20, transcendentals=0
)


def columns(width):
    return [(at, min(CHUNK, width - at)) for at in range(0, width, CHUNK)]


def times_basis(rows, basis):
    return lax.dot_general(
        rows, basis, (((1,), (1,)), ((), ())), preferred_element_type=jnp.float32
    )


def ref_kernel(x_hbm, g_hbm, bx_hbm, bg_hbm, z_ref, bx, bg, x, g, sems):
    work = []
    for part, (src, basis_src, dst, basis_dst) in enumerate(
        ((x_hbm, bx_hbm, x, bx), (g_hbm, bg_hbm, g, bg))
    ):
        for at, step in columns(src.shape[2]):
            cut = pl.ds(at, step)
            k = len(work)
            copies = (
                pltpu.make_async_copy(basis_src.at[:, cut], basis_dst.at[:, cut], sems.at[0, k]),
                pltpu.make_async_copy(src.at[0, :, cut], dst.at[:, cut], sems.at[1, k]),
            )
            for copy in copies:
                copy.start()
            work.append((part, dst, basis_dst, cut, copies))
    sums = [None, None]
    for part, rows, basis, cut, copies in work:
        for copy in copies:
            copy.wait()
        term = times_basis(rows[:, cut], basis[:, cut])
        sums[part] = term if sums[part] is None else sums[part] + term
    z_ref[...] = jnp.concatenate([sums[1], sums[0]], axis=1)


def project_ref(x, g, bx, bg):
    span, wide_x, wide_g = x.shape[1], x.shape[2], g.shape[2]
    parts = len(columns(wide_x)) + len(columns(wide_g))
    return pl.pallas_call(
        ref_kernel,
        out_shape=(
            jax.ShapeDtypeStruct((span, bx.shape[0] + bg.shape[0]), jnp.float32),
            jax.ShapeDtypeStruct(bx.shape, bx.dtype),
            jax.ShapeDtypeStruct(bg.shape, bg.dtype),
        ),
        in_specs=[pl.BlockSpec(memory_space=pl.ANY)] * 4,
        out_specs=(pl.BlockSpec(memory_space=pltpu.VMEM),) * 3,
        scratch_shapes=[
            pltpu.VMEM((span, wide_x), x.dtype),
            pltpu.VMEM((span, wide_g), g.dtype),
            pltpu.SemaphoreType.DMA((2, parts)),
        ],
        compiler_params=pltpu.CompilerParams(vmem_limit_bytes=REF_ROOM),
        cost_estimate=ROOM_FOR_PREFETCH,
    )(*(pltpu.with_memory_space_constraint(a, pltpu.HBM) for a in (x, g, bx, bg)))


def sketch_of(z):
    half = z.shape[1] // 2
    full = lax.dot_general(
        z[:, :half], z[:, half:], (((0,), (0,)), ((), ())),
        preferred_element_type=jnp.float32, precision=EXACT,
    )
    rows = half // 2
    return jnp.concatenate([full[:rows], full[rows:]], axis=1)


def sketch_kernel(len_ref, own_ref, other_ref, sketch_ref):
    z = own_ref[...] + other_ref[...]
    keep = lax.broadcasted_iota(jnp.int32, z.shape, 0) < len_ref[0]
    sketch_ref[...] = sketch_of(jnp.where(keep, z, 0.0))


def ref_sketch(length, own, other):
    half = own.shape[1] // 2
    return pl.pallas_call(
        sketch_kernel,
        out_shape=jax.ShapeDtypeStruct((half // 2, half * 2), jnp.float32),
        in_specs=[pl.BlockSpec(memory_space=pltpu.SMEM)]
        + [pl.BlockSpec(memory_space=pltpu.VMEM)] * 2,
        out_specs=pl.BlockSpec(memory_space=pltpu.VMEM),
        compiler_params=pltpu.CompilerParams(vmem_limit_bytes=8 << 20),
        cost_estimate=ROOM_FOR_PREFETCH,
    )(length, own, other)


def roll_kernel(after_ref, len_ref, x_ref, g_ref, bx_ref, bg_ref, z_ref):
    rolls, span, _ = x_ref.shape
    row = len_ref[...]
    lens = [row[i] for i in range(rolls)]
    half = bg_ref.shape[0]

    @pl.loop(0, rolls)
    def _(roll):
        length = sum(jnp.where(roll == i, lens[i], 0) for i in range(rolls))
        need = (length + (TILE - 1)) // TILE
        for tiles in range(1, span // TILE + 1):

            @pl.when(need == tiles)
            def _():
                rows = pl.ds(0, tiles * TILE)
                for k, (src, basis) in enumerate(((g_ref, bg_ref), (x_ref, bx_ref))):
                    z_ref[roll, rows, k * half : (k + 1) * half] = times_basis(
                        src[roll, rows, :], basis[...]
                    )


def project_rolls(operands):
    rolls, span, wide_x = operands[2].shape
    wide_g, width = operands[3].shape[2], operands[4].shape[0] * 2
    held = pl.BlockSpec(memory_space=pltpu.VMEM)
    return pl.pallas_call(
        roll_kernel,
        out_shape=jax.ShapeDtypeStruct((rolls, span, width), jnp.float32),
        in_specs=[pl.BlockSpec(memory_space=pl.ANY)] + [held] * 5,
        out_specs=held,
        compiler_params=pltpu.CompilerParams(vmem_limit_bytes=ROLL_ROOM),
        cost_estimate=pl.CostEstimate(
            flops=rolls * span * (wide_x + wide_g) * width,
            bytes_accessed=12 << 20,
            transcendentals=0,
        ),
    )(*operands)


def units_kernel(lens, own_ref, other_ref, unit_ref):
    row = lens[...]
    rolls = [row[i] for i in range(lens.shape[0])]
    for roll, length in enumerate(rolls):
        z = own_ref[roll] + other_ref[roll]
        keep = lax.broadcasted_iota(jnp.int32, z.shape, 0) < length
        sketch = sketch_of(jnp.where(keep, z, 0.0))
        square = jnp.sum(sketch * sketch, axis=(0, 1), keepdims=True)
        size = sketch.shape[0] * sketch.shape[1]
        unit_ref[roll] = sketch / (jnp.sqrt(square / size + 1e-6) * math.sqrt(size))


def roll_units(lengths, own, other):
    rolls = lengths.shape[0]
    half = own.shape[2] // 2
    return pl.pallas_call(
        units_kernel,
        out_shape=jax.ShapeDtypeStruct((rolls, half // 2, half * 2), jnp.float32),
        in_specs=[pl.BlockSpec(memory_space=pltpu.VMEM)] * 3,
        out_specs=pl.BlockSpec(memory_space=pltpu.VMEM),
        compiler_params=pltpu.CompilerParams(vmem_limit_bytes=8 << 20),
    )(lengths, own, other)


def score_kernel(order, dp_axis, unit_ref, *refs):
    sketch_refs, out_ref = refs[:-1], refs[-1]
    rolls = unit_ref.shape[0]
    total = len(order)
    me = lax.axis_index(dp_axis)
    lanes = unit_ref.shape[2]
    place = lax.broadcasted_iota(jnp.int32, (total, lanes), 0)
    tables = [jnp.zeros((total, lanes), jnp.float32) for _ in range(rolls + 1)]
    size = unit_ref.shape[1] * lanes
    at = 0
    for ref in sketch_refs:
        for i in range(ref.shape[0]):
            sketch = ref[i]
            here = place == jnp.bitwise_xor(me, order[at])
            for k in range(rolls + 1):
                other = unit_ref[k] if k < rolls else sketch
                row = jnp.sum(sketch * other, axis=0, keepdims=True)
                tables[k] = jnp.where(here, row, tables[k])
            at += 1
    ones = jnp.ones((8, lanes), jnp.float32)
    added = [
        lax.dot_general(
            ones, table, (((1,), (1,)), ((), ())),
            preferred_element_type=jnp.float32, precision=EXACT,
        )
        for table in tables
    ]
    spread = jnp.sqrt(added[rolls] / size + 1e-6)
    out_ref[...] = jnp.concatenate([(added[k] / spread)[0:1] for k in range(rolls)], axis=0)


def score(units, sketches, order):
    return pl.pallas_call(
        functools.partial(score_kernel, order, "dp"),
        out_shape=jax.ShapeDtypeStruct((units.shape[0], len(order)), jnp.float32),
        in_specs=[pl.BlockSpec(memory_space=pltpu.VMEM)] * (1 + len(sketches)),
        out_specs=pl.BlockSpec(memory_space=pltpu.VMEM),
        compiler_params=pltpu.CompilerParams(vmem_limit_bytes=8 << 20),
    )(units, *sketches)


def other_core(value):
    return lax.ppermute(value, "tensor", [(0, 1), (1, 0)])


def from_chip(value, bit, devices, cores):
    pairs = [
        (i * cores + t, (i ^ bit) * cores + (t + 1) % cores)
        for i in range(devices)
        for t in range(cores)
    ]
    return lax.ppermute(value, ("dp", "tensor"), pairs)


def on_device(
    devices, cores, roll_inputs, roll_grads, ref_inputs, ref_grads, in_basis, out_basis,
    roll_lengths, ref_lengths,
):
    bx, bg = in_basis.T, out_basis.T
    ref_z, bx, bg = project_ref(ref_inputs, ref_grads, bx, bg)
    sketch = ref_sketch(ref_lengths, ref_z, other_core(ref_z))

    held = sketch[None]
    order = [0]
    bits = [1 << k for k in range(devices.bit_length() - 1)]
    turns = (bits[1], bits[2], bits[1] ^ bits[2])
    got = [from_chip(held, turn, devices, cores) for turn in turns]
    z = project_rolls((held, roll_lengths, roll_inputs, roll_grads, bx, bg))
    *got, z = lax.optimization_barrier((*got, z))
    order = order + [k ^ turn for turn in turns for k in order]
    for bit in bits[:1] + bits[3:]:
        held = jnp.concatenate([held, *got], axis=0)
        got = [from_chip(held, bit, devices, cores)]
        order = order + [k ^ bit for k in order]
    units = roll_units(roll_lengths, z, other_core(z))
    return score(units, (held, *got), tuple(order))


def solution(mesh):
    placed = (
        P(("group", "dp"), None, "tensor"),
        P(("group", "dp"), None, "tensor"),
        P(("group", "dp"), None, "tensor"),
        P(("group", "dp"), None, "tensor"),
        P("tensor", None),
        P("tensor", None),
        P(("group", "dp")),
        P(("group", "dp")),
    )
    return jax.shard_map(
        functools.partial(on_device, mesh.shape["dp"], mesh.shape["tensor"]),
        mesh=mesh,
        in_specs=placed,
        out_specs=P(("group", "dp"), None),
        check_vma=False,
    )
```
